512 devices in a mesh: ctx: 128 (over z, y, core), head: 4 (over x).
Axes of the slice: x: 4, y: 4, z: 16, core: 2. Of those that a mesh axis runs over, the one named last changes fastest.
Arguments:
- inputs: bfloat16 [16384, 3584], P('ctx', 'head'), may hold values from -9 to 9
- queries: bfloat16 [16384, 3584], P('ctx', 'head'), may hold values from -8 to 8
- w_key: bfloat16 [3584, 512], P(None, 'head'), may hold values from -1.5 to 1.5
- w_value: bfloat16 [3584, 512], P(None, 'head'), may hold values from -0.09375 to 0.09375
- v_bias: bfloat16 [512], P('head'), may hold values from -6 to 6
- cotangent: bfloat16 [16384, 3584], P('ctx', 'head'), may hold values from -96 to 96
Outputs:
- attended: bfloat16 [16384, 3584], P('ctx', 'head')
- query_grad: bfloat16 [16384, 3584], P('ctx', 'head')
- input_grad: bfloat16 [16384, 3584], P('ctx', 'head')
The draws below stay inside these ranges and needn't reach their ends.
All inputs are finite; a program needn't handle non-finite values.
Results may differ from the reference program's by a relative error of at most 0.025.
Values may be sent and summed in bfloat16 or wider, within the bound.
No kernel may reach another device: no remote copies, remote signals or barrier semaphores. Data moves between devices by JAX's collectives and lax.ppermute only.
A program may use at most 64 MiB of HBM per device.

```python
import math
import jax
import jax.numpy as jnp
from jax import lax

D = 3584
HEADS = 28
HEADS_KV = 4
HEAD_DIM = 128
BLOCK = 128
SEQ = 16384


def draw_inputs(key, part):
    key = jax.random.fold_in(key, 11)
    base_key = jax.random.fold_in(key, 0)
    result = jnp.clip(jax.random.normal(base_key, (SEQ, D), jnp.float32), -6.0, 6.0)
    return result.astype(jnp.bfloat16)


def draw_queries(key, part):
    key = jax.random.fold_in(key, 12)
    base_key = jax.random.fold_in(key, 0)
    result = jnp.clip(jax.random.normal(base_key, (SEQ, HEADS * HEAD_DIM), jnp.float32), -6.0, 6.0)
    return result.astype(jnp.bfloat16)


def draw_w_key(key, part):
    key = jax.random.fold_in(key, 13)
    result = jnp.clip(jax.random.normal(key, (D, HEADS_KV * HEAD_DIM), jnp.float32), -6.0, 6.0) / math.sqrt(D)
    return result.astype(jnp.bfloat16)


def steps_of(own_key, extent, pieces, low, top_value):
    gain = 1.0
    for dim, parts in pieces:
        steps = jax.random.uniform(jax.random.fold_in(jax.random.fold_in(own_key, 6), dim), (parts,), jnp.float32, low / len(pieces), top_value / len(pieces))
        gain = gain * jnp.repeat(jnp.exp(steps), extent[dim] // parts).reshape((-1,) + (1,) * (len(extent) - 1 - dim))
    return gain


def gaussian(rng, shape, width, bound, pieces=(), held_as=jnp.bfloat16):
    level = steps_of(rng, shape, pieces, -0.22, 0.18) if pieces else 1.0
    values = jax.random.normal(rng, shape, jnp.float32) * width * level
    return jnp.minimum(jnp.maximum(values, -bound), bound).astype(held_as)


def setup_inputs(seed: int = 0) -> dict:
    key_of = jax.random.split(jax.random.key(seed), 7)
    inputs = draw_inputs(jax.random.fold_in(key_of[6], 71), 0)
    queries = draw_queries(jax.random.fold_in(key_of[6], 71), 0)
    w_key = draw_w_key(jax.random.fold_in(key_of[6], 71), 0)
    w_value = gaussian(key_of[3], (D, HEADS_KV * HEAD_DIM), D ** -0.5, 0.09375, ((1, 4),))
    v_bias = gaussian(key_of[4], (HEADS_KV * HEAD_DIM,), 1.0, 6.0, ((0, 4),))
    cotangent = gaussian(key_of[5], (SEQ, HEADS * HEAD_DIM), 16.0, 96.0, ((0, 128), (1, 4)))
    return {"inputs": inputs, "queries": queries, "w_key": w_key, "w_value": w_value, "v_bias": v_bias, "cotangent": cotangent}


def block_distances(block_count):
    listed = [0]
    stride = 1
    while stride < block_count:
        listed.append(stride)
        stride = stride * 2
    return listed

def reference(inputs, queries, w_key, w_value, v_bias, cotangent):
    keys_all = jnp.dot(inputs, w_key, preferred_element_type=jnp.float32).astype(jnp.bfloat16)
    values_all = (jnp.dot(inputs, w_value, preferred_element_type=jnp.float32) + v_bias.astype(jnp.float32)).astype(jnp.bfloat16)
    block_count = SEQ // BLOCK
    group_size = HEADS // HEADS_KV
    inverse_root = 1.0 / math.sqrt(HEAD_DIM)
    listed = block_distances(block_count)
    level_count = len(listed)
    offsets = jnp.array(listed, dtype=jnp.int32)
    key_blocks = keys_all.reshape(block_count, BLOCK, HEADS_KV, HEAD_DIM)
    value_blocks = values_all.reshape(block_count, BLOCK, HEADS_KV, HEAD_DIM)
    query_blocks = queries.reshape(block_count, BLOCK, HEADS_KV, group_size, HEAD_DIM)
    grad_blocks = cotangent.reshape(block_count, BLOCK, HEADS_KV, group_size, HEAD_DIM)
    causal = jnp.arange(BLOCK)[:, None] >= jnp.arange(BLOCK)[None, :]
    first_level = (jnp.arange(level_count) == 0)[None, :, None]

    def one_block(carry, position):
        key_total, value_total = carry
        sources = position - offsets
        valid_rows = sources >= 0
        sources = jnp.maximum(sources, 0).astype(jnp.int32)
        key_rows = key_blocks[sources].astype(jnp.float32)
        value_rows = value_blocks[sources].astype(jnp.float32)
        query_rows = query_blocks[position].astype(jnp.float32)
        grad_rows = grad_blocks[position].astype(jnp.float32)
        allowed = jnp.where(first_level, causal[:, None, :], valid_rows[None, :, None])
        scores = jnp.einsum('qgrd,lkgd->grqlk', query_rows, key_rows) * inverse_root
        scores = jnp.where(allowed, scores, -jnp.inf)
        row_top = lax.optimization_barrier(jnp.max(scores, axis=(3, 4), keepdims=True))
        log_total = row_top + jnp.log(lax.optimization_barrier(jnp.sum(jnp.exp(scores - row_top), axis=(3, 4), keepdims=True)))
        prob_rows = jnp.exp(scores - log_total)
        weights = lax.optimization_barrier(prob_rows.astype(jnp.bfloat16)).astype(jnp.float32)
        attended = jnp.einsum('grqlk,lkgd->qgrd', weights, value_rows).astype(jnp.bfloat16)
        attended_wide = lax.optimization_barrier(attended).astype(jnp.float32)
        deltas = jnp.transpose(lax.optimization_barrier(jnp.sum(grad_rows * attended_wide, axis=-1)), (1, 2, 0))
        dprobs = jnp.einsum('qgrd,lkgd->grqlk', grad_rows, value_rows)
        dscores = lax.optimization_barrier((prob_rows * (dprobs - deltas[:, :, :, None, None])).astype(jnp.bfloat16)).astype(jnp.float32)
        query_grad = (jnp.einsum('grqlk,lkgd->qgrd', dscores, key_rows) * inverse_root).astype(jnp.bfloat16)
        key_grad = jnp.einsum('grqlk,qgrd->lkgd', dscores, query_rows) * inverse_root
        value_grad = jnp.einsum('grqlk,qgrd->lkgd', weights, grad_rows)
        key_total = key_total.at[sources].add(key_grad)
        value_total = value_total.at[sources].add(value_grad)
        return ((key_total, value_total), (attended, query_grad))
    zero_total = jnp.zeros((block_count, BLOCK, HEADS_KV, HEAD_DIM), jnp.float32)
    totals, stacked = lax.scan(one_block, (zero_total, zero_total), jnp.arange(block_count, dtype=jnp.int32))
    key_total, value_total = totals
    attended_all, query_all = stacked
    attended_out = attended_all.reshape(SEQ, HEADS * HEAD_DIM)
    query_out = query_all.reshape(SEQ, HEADS * HEAD_DIM)
    key_final = key_total.reshape(SEQ, HEADS_KV * HEAD_DIM).astype(jnp.bfloat16)
    value_final = value_total.reshape(SEQ, HEADS_KV * HEAD_DIM).astype(jnp.bfloat16)
    contract = (((1,), (1,)), ((), ()))
    input_terms = lax.dot_general(key_final, w_key, contract, preferred_element_type=jnp.float32)
    input_terms = input_terms + lax.dot_general(value_final, w_value, contract, preferred_element_type=jnp.float32)
    return (attended_out, query_out, input_terms.astype(jnp.bfloat16))
```

```python
import functools
import math

import jax
import jax.numpy as jnp
from jax import lax
from jax.experimental import pallas as pl
from jax.experimental.pallas import tpu as pltpu
from jax.sharding import PartitionSpec as P

HEAD_DIM = 128
BLOCK = 128
DIMS_NT = (((1,), (1,)), ((), ()))
DIMS_TN = (((0,), (0,)), ((), ()))
DIMS_NN = (((1,), (0,)), ((), ()))
SCALE = 1.0 / math.sqrt(HEAD_DIM)
VMEM = pl.BlockSpec(memory_space=pltpu.VMEM)
SMEM = pl.BlockSpec(memory_space=pltpu.SMEM)


def dot(a, b, dims):
    return lax.dot_general(a, b, dims, preferred_element_type=jnp.float32)


def project_kernel(x_ref, wk_ref, wv_ref, bias_ref, kv_ref):
    rows = x_ref[...]
    keys = dot(rows, wk_ref[...], DIMS_NN)
    values = dot(rows, wv_ref[...], DIMS_NN) + bias_ref[...].astype(jnp.float32)
    kv_ref[:, :HEAD_DIM] = keys.astype(jnp.bfloat16)
    kv_ref[:, HEAD_DIM:] = values.astype(jnp.bfloat16)


def attention_kernel(
    place_ref, q_ref, c_ref, own_ref, sib_ref, r1_ref, r2_ref, r3_ref, sw_ref,
    att_ref, dq_ref, local_ref, near_ref, far_ref,
    keys, values, weights, dscores,
):
    place = place_ref[0]
    core = lax.rem(place, 2)
    group = q_ref.shape[1] // HEAD_DIM
    B = BLOCK
    first = jnp.where(core == 0, sw_ref[2 * B : 3 * B, :], sib_ref[...])
    parts = [own_ref[...], first, r1_ref[:B, :], r2_ref[:B, :], r3_ref[:B, :]]
    parts += [sw_ref[:B, :], sw_ref[B : 2 * B, :], sw_ref[3 * B :, :]]
    for slot, part in enumerate(parts):
        keys[slot * B : (slot + 1) * B, :] = part[:, :HEAD_DIM]
        values[slot * B : (slot + 1) * B, :] = part[:, HEAD_DIM:]
    near, far = jnp.int32(1) - core, core
    steps = [jnp.int32(1)]
    steps += [lax.shift_left(jnp.int32(1), bit + near) for bit in (5, 3, 1)]
    steps += [lax.shift_left(jnp.int32(1), bit + far) for bit in (5, 3, 1)]
    causal = lax.broadcasted_iota(jnp.int32, (B, B), 0) >= lax.broadcasted_iota(jnp.int32, (B, B), 1)
    penalty = [jnp.where(place >= step, 0.0, -jnp.inf).astype(jnp.float32) for step in steps]
    all_keys = keys[...]
    all_values = values[...]
    for head in range(group):
        cols = slice(head * HEAD_DIM, (head + 1) * HEAD_DIM)
        rows = slice(head * B, (head + 1) * B)
        query = q_ref[:, cols]
        grad = c_ref[:, cols]
        raw = dot(query, all_keys, DIMS_NT) * SCALE
        pieces = [jnp.where(causal, raw[:, :B], -jnp.inf)]
        for slot in range(1, 8):
            pieces.append(raw[:, slot * B : (slot + 1) * B] + penalty[slot - 1])
        scores = jnp.concatenate(pieces, axis=1)
        top = jnp.max(scores, axis=1, keepdims=True)
        raised = jnp.exp(scores - top)
        prob = raised * (1.0 / jnp.sum(raised, axis=1, keepdims=True))
        weight = prob.astype(jnp.bfloat16)
        weights[rows, :] = weight
        attended = dot(weight, all_values, DIMS_NN).astype(jnp.bfloat16)
        att_ref[:, cols] = attended
        delta = jnp.sum(
            grad.astype(jnp.float32) * attended.astype(jnp.float32), axis=1, keepdims=True
        )
        dprob = dot(grad, all_values, DIMS_NT)
        dscore = (prob * (dprob - delta)).astype(jnp.bfloat16)
        dscores[rows, :] = dscore
        dq_ref[:, cols] = (dot(dscore, all_keys, DIMS_NN) * SCALE).astype(jnp.bfloat16)
    queries = jnp.concatenate(
        [q_ref[:, h * HEAD_DIM : (h + 1) * HEAD_DIM] for h in range(group)], axis=0
    )
    grads = jnp.concatenate(
        [c_ref[:, h * HEAD_DIM : (h + 1) * HEAD_DIM] for h in range(group)], axis=0
    )
    for slot in range(8):
        cols = slice(slot * B, (slot + 1) * B)
        dkey = dot(dscores[:, cols], queries, DIMS_TN) * SCALE
        dvalue = dot(weights[:, cols], grads, DIMS_TN)
        if slot == 0:
            local_ref[:, :HEAD_DIM] = dkey
            local_ref[:, HEAD_DIM:] = dvalue
        else:
            target, row = (near_ref, slot - 2) if 2 <= slot < 5 else (far_ref, slot - 5)
            if slot == 1:
                target, row = far_ref, 3
            target[row * B : (row + 1) * B, :HEAD_DIM] = dkey.astype(jnp.bfloat16)
            target[row * B : (row + 1) * B, HEAD_DIM:] = dvalue.astype(jnp.bfloat16)


def finish_kernel(place_ref, local_ref, swap_ref, a1_ref, a2_ref, a3_ref, t_ref, wk_ref, wv_ref, out_ref):
    core = lax.rem(place_ref[0], 2)
    B = BLOCK
    total = local_ref[...]
    total += jnp.where(core == 0, swap_ref[3 * B :, :].astype(jnp.float32), 0.0)
    for ref in (a1_ref, a2_ref, a3_ref):
        total += ref[:B, :].astype(jnp.float32)
    total = (total + t_ref[...].astype(jnp.float32)).astype(jnp.bfloat16)
    width = wk_ref.shape[0] // 4
    for part in range(4):
        rows = slice(part * width, (part + 1) * width)
        term = dot(total[:, :HEAD_DIM], wk_ref[rows, :], DIMS_NT)
        term += dot(total[:, HEAD_DIM:], wv_ref[rows, :], DIMS_NT)
        out_ref[part * B : (part + 1) * B, :] = term.astype(jnp.bfloat16)


def add_kernel(parts_ref, out_ref):
    B = BLOCK
    total = parts_ref[:B, :].astype(jnp.float32)
    for part in range(1, 4):
        total += parts_ref[part * B : (part + 1) * B, :].astype(jnp.float32)
    out_ref[...] = total.astype(jnp.bfloat16)


def call(kernel, out_shape, args, scratch=(), flops=0):
    specs = [SMEM if a.dtype == jnp.int32 else VMEM for a in args]
    return pl.pallas_call(
        kernel,
        out_shape=out_shape,
        in_specs=specs,
        out_specs=jax.tree.map(lambda _: VMEM, out_shape),
        scratch_shapes=list(scratch),
        compiler_params=pltpu.CompilerParams(vmem_limit_bytes=30 * 1024 * 1024),
        cost_estimate=pl.CostEstimate(
            flops=flops,
            bytes_accessed=sum(a.size * a.dtype.itemsize for a in args),
            transcendentals=0,
        ),
    )(*args)


def swap(value, count):
    return lax.ppermute(value, "ctx", [(i, i ^ 1) for i in range(count)])


def shift(value, count, even, odd):
    pairs = []
    for i in range(count):
        to = i + (even if i % 2 == 0 else odd)
        if 0 <= to < count:
            pairs.append((i, to))
    return lax.ppermute(value, "ctx", pairs)


def shards(inputs, queries, w_key, w_value, v_bias, cotangent):
    count = lax.axis_size("ctx")
    place = lax.axis_index("ctx").astype(jnp.int32).reshape(1)
    B = BLOCK
    bf16 = jnp.bfloat16
    width = queries.shape[1]
    rows = lax.all_gather(inputs, "head", axis=1, tiled=True)
    own = call(
        project_kernel,
        jax.ShapeDtypeStruct((B, 2 * HEAD_DIM), bf16),
        (rows, w_key, w_value, v_bias.reshape(1, HEAD_DIM)),
        flops=4 * B * rows.shape[1] * HEAD_DIM,
    )
    sibling = swap(own, count)
    pair = jnp.concatenate([own, sibling], axis=0)
    r1 = shift(pair, count, 64, 32)
    r2 = shift(pair, count, 16, 8)
    r3 = shift(pair, count, 4, 2)
    swapped = swap(jnp.concatenate([r1[B:], r2[B:], r3], axis=0), count)
    attended, query_grad, local, near, far = call(
        attention_kernel,
        (
            jax.ShapeDtypeStruct((B, width), bf16),
            jax.ShapeDtypeStruct((B, width), bf16),
            jax.ShapeDtypeStruct((B, 2 * HEAD_DIM), jnp.float32),
            jax.ShapeDtypeStruct((3 * B, 2 * HEAD_DIM), bf16),
            jax.ShapeDtypeStruct((4 * B, 2 * HEAD_DIM), bf16),
        ),
        (place, queries, cotangent, own, sibling, r1, r2, r3, swapped),
        scratch=(
            pltpu.VMEM((8 * B, HEAD_DIM), bf16),
            pltpu.VMEM((8 * B, HEAD_DIM), bf16),
            pltpu.VMEM((width, 8 * B), bf16),
            pltpu.VMEM((width, 8 * B), bf16),
        ),
        flops=12 * width * 8 * B * HEAD_DIM,
    )
    back = swap(far, count)
    m1 = jnp.concatenate([near[:B], back[:B]], axis=0)
    m2 = jnp.concatenate([near[B : 2 * B], back[B : 2 * B]], axis=0)
    extra = jnp.where(place[0] % 2 == 1, back[3 * B :].astype(jnp.float32), 0.0)
    third = (near[2 * B :].astype(jnp.float32) + extra).astype(bf16)
    m3 = jnp.concatenate([third, back[2 * B : 3 * B]], axis=0)
    a1 = shift(m1, count, -64, -32)
    a2 = shift(m2, count, -16, -8)
    a3 = shift(m3, count, -4, -2)
    across = a1[B:].astype(jnp.float32) + a2[B:].astype(jnp.float32) + a3[B:].astype(jnp.float32)
    last = swap(across.astype(bf16), count)
    terms = call(
        finish_kernel,
        jax.ShapeDtypeStruct((4 * B, width), bf16),
        (place, local, back, a1, a2, a3, last, w_key, w_value),
        flops=4 * B * 4 * width * HEAD_DIM,
    )
    arrived = lax.all_to_all(terms, "head", 0, 0, tiled=True)
    input_grad = call(add_kernel, jax.ShapeDtypeStruct((B, width), bf16), (arrived,))
    return (attended, query_grad, input_grad)


def solution(mesh):
    return jax.shard_map(
        shards,
        mesh=mesh,
        in_specs=(
            P("ctx", "head"),
            P("ctx", "head"),
            P(None, "head"),
            P(None, "head"),
            P("head"),
            P("ctx", "head"),
        ),
        out_specs=(P("ctx", "head"), P("ctx", "head"), P("ctx", "head")),
        check_vma=False,
    )
```

```python
import functools
import math

import jax
import jax.numpy as jnp
from jax import lax
from jax.experimental import pallas as pl
from jax.experimental.pallas import tpu as pltpu
from jax.sharding import PartitionSpec as P

HEAD_DIM = 128
BLOCK = 128
DIMS_NT = (((1,), (1,)), ((), ()))
DIMS_TN = (((0,), (0,)), ((), ()))
DIMS_NN = (((1,), (0,)), ((), ()))
SCALE = 1.0 / math.sqrt(HEAD_DIM)
VMEM = pl.BlockSpec(memory_space=pltpu.VMEM)
SMEM = pl.BlockSpec(memory_space=pltpu.SMEM)


def dot(a, b, dims):
    return lax.dot_general(a, b, dims, preferred_element_type=jnp.float32)


def project_kernel(x_ref, wk_hbm, wv_hbm, bias_hbm, kv_ref, wk, wv, bias, sems):
    pairs = [(wk_hbm, wk), (bias_hbm, bias), (wv_hbm, wv)]
    copies = [pltpu.make_async_copy(a, b, sems.at[i]) for i, (a, b) in enumerate(pairs)]
    for copy in copies:
        copy.start()
    rows = x_ref[...]
    copies[0].wait()
    kv_ref[:, :HEAD_DIM] = dot(rows, wk[...], DIMS_NN).astype(jnp.bfloat16)
    copies[1].wait()
    copies[2].wait()
    values = dot(rows, wv[...], DIMS_NN) + bias[...].astype(jnp.float32)
    kv_ref[:, HEAD_DIM:] = values.astype(jnp.bfloat16)


def half_kernel(r1_ref, out_ref):
    out_ref[...] = r1_ref[BLOCK:, :]


def join_kernel(s1_ref, r2_ref, out_ref):
    out_ref[:BLOCK, :] = s1_ref[...]
    out_ref[BLOCK:, :] = r2_ref[BLOCK:, :]


def pack_kernel(s12_ref, r3_ref, out_ref):
    out_ref[: 2 * BLOCK, :] = s12_ref[...]
    out_ref[2 * BLOCK :, :] = r3_ref[...]


def attention_kernel(
    place_ref, q_ref, c_ref, own_ref, sib_ref, r1_ref, r2_ref, r3_ref, sw_ref,
    att_ref, dq_ref, local_ref, near_ref, far_ref,
    keys, values, weights, dscores,
):
    place = place_ref[0]
    core = lax.rem(place, 2)
    group = q_ref.shape[1] // HEAD_DIM
    B = BLOCK
    first = jnp.where(core == 0, sw_ref[2 * B : 3 * B, :], sib_ref[...])
    parts = [own_ref[...], first, r1_ref[:B, :], r2_ref[:B, :], r3_ref[:B, :]]
    parts += [sw_ref[:B, :], sw_ref[B : 2 * B, :], sw_ref[3 * B :, :]]
    for slot, part in enumerate(parts):
        keys[slot * B : (slot + 1) * B, :] = part[:, :HEAD_DIM]
        values[slot * B : (slot + 1) * B, :] = part[:, HEAD_DIM:]
    near, far = jnp.int32(1) - core, core
    steps = [jnp.int32(1)]
    steps += [lax.shift_left(jnp.int32(1), bit + near) for bit in (5, 3, 1)]
    steps += [lax.shift_left(jnp.int32(1), bit + far) for bit in (5, 3, 1)]
    causal = lax.broadcasted_iota(jnp.int32, (B, B), 0) >= lax.broadcasted_iota(jnp.int32, (B, B), 1)
    penalty = [jnp.where(place >= step, 0.0, -jnp.inf).astype(jnp.float32) for step in steps]
    all_keys = keys[...]
    all_values = values[...]
    for head in range(group):
        cols = slice(head * HEAD_DIM, (head + 1) * HEAD_DIM)
        rows = slice(head * B, (head + 1) * B)
        query = q_ref[:, cols]
        grad = c_ref[:, cols]
        raw = dot(query, all_keys, DIMS_NT) * SCALE
        pieces = [jnp.where(causal, raw[:, :B], -jnp.inf)]
        for slot in range(1, 8):
            pieces.append(raw[:, slot * B : (slot + 1) * B] + penalty[slot - 1])
        scores = jnp.concatenate(pieces, axis=1)
        top = jnp.max(scores, axis=1, keepdims=True)
        raised = jnp.exp(scores - top)
        prob = raised * (1.0 / jnp.sum(raised, axis=1, keepdims=True))
        weight = prob.astype(jnp.bfloat16)
        weights[rows, :] = weight
        attended = dot(weight, all_values, DIMS_NN).astype(jnp.bfloat16)
        att_ref[:, cols] = attended
        delta = jnp.sum(
            grad.astype(jnp.float32) * attended.astype(jnp.float32), axis=1, keepdims=True
        )
        dprob = dot(grad, all_values, DIMS_NT)
        dscore = (prob * (dprob - delta)).astype(jnp.bfloat16)
        dscores[rows, :] = dscore
        dq_ref[:, cols] = (dot(dscore, all_keys, DIMS_NN) * SCALE).astype(jnp.bfloat16)
    queries = jnp.concatenate(
        [q_ref[:, h * HEAD_DIM : (h + 1) * HEAD_DIM] for h in range(group)], axis=0
    )
    grads = jnp.concatenate(
        [c_ref[:, h * HEAD_DIM : (h + 1) * HEAD_DIM] for h in range(group)], axis=0
    )
    for slot in range(8):
        cols = slice(slot * B, (slot + 1) * B)
        dkey = dot(dscores[:, cols], queries, DIMS_TN) * SCALE
        dvalue = dot(weights[:, cols], grads, DIMS_TN)
        if slot == 0:
            local_ref[:, :HEAD_DIM] = dkey
            local_ref[:, HEAD_DIM:] = dvalue
        else:
            target, row = (near_ref, slot - 2) if 2 <= slot < 5 else (far_ref, slot - 5)
            if slot == 1:
                target, row = far_ref, 3
            target[row * B : (row + 1) * B, :HEAD_DIM] = dkey.astype(jnp.bfloat16)
            target[row * B : (row + 1) * B, HEAD_DIM:] = dvalue.astype(jnp.bfloat16)


def finish_kernel(place_ref, local_ref, swap_ref, a1_ref, a2_ref, a3_ref, t_ref, wk_ref, wv_ref, out_ref):
    core = lax.rem(place_ref[0], 2)
    B = BLOCK
    total = local_ref[...]
    total += jnp.where(core == 0, swap_ref[3 * B :, :].astype(jnp.float32), 0.0)
    for ref in (a1_ref, a2_ref, a3_ref):
        total += ref[:B, :].astype(jnp.float32)
    total = (total + t_ref[...].astype(jnp.float32)).astype(jnp.bfloat16)
    width = wk_ref.shape[0] // 4
    for part in range(4):
        rows = slice(part * width, (part + 1) * width)
        term = dot(total[:, :HEAD_DIM], wk_ref[rows, :], DIMS_NT)
        term += dot(total[:, HEAD_DIM:], wv_ref[rows, :], DIMS_NT)
        out_ref[part * B : (part + 1) * B, :] = term.astype(jnp.bfloat16)


def add_kernel(parts_ref, out_ref):
    B = BLOCK
    total = parts_ref[:B, :].astype(jnp.float32)
    for part in range(1, 4):
        total += parts_ref[part * B : (part + 1) * B, :].astype(jnp.float32)
    out_ref[...] = total.astype(jnp.bfloat16)


def out_spec(shape):
    return VMEM if isinstance(shape, jax.ShapeDtypeStruct) else pl.BlockSpec(memory_space=pltpu.HBM)


def call(kernel, out_shape, args, scratch=(), flops=0, hbm=()):
    specs = [SMEM if a.dtype == jnp.int32 else VMEM for a in args]
    for index in hbm:
        specs[index] = pl.BlockSpec(memory_space=pltpu.HBM)
    args = [
        pltpu.with_memory_space_constraint(a, pltpu.HBM) if i in hbm else a
        for i, a in enumerate(args)
    ]
    return pl.pallas_call(
        kernel,
        out_shape=out_shape,
        in_specs=specs,
        out_specs=jax.tree.map(out_spec, out_shape),
        scratch_shapes=list(scratch),
        compiler_params=pltpu.CompilerParams(vmem_limit_bytes=30 * 1024 * 1024),
        cost_estimate=pl.CostEstimate(
            flops=flops,
            bytes_accessed=sum(a.size * a.dtype.itemsize for a in args),
            transcendentals=0,
        ),
    )(*args)


def swap(value, count):
    return lax.ppermute(value, "ctx", [(i, i ^ 1) for i in range(count)])


def shift(value, count, even, odd):
    pairs = []
    for i in range(count):
        to = i + (even if i % 2 == 0 else odd)
        if 0 <= to < count:
            pairs.append((i, to))
    return lax.ppermute(value, "ctx", pairs)


def shards(inputs, queries, w_key, w_value, v_bias, cotangent):
    count = lax.axis_size("ctx")
    place = lax.axis_index("ctx").astype(jnp.int32).reshape(1)
    B = BLOCK
    bf16 = jnp.bfloat16
    width = queries.shape[1]
    rows = lax.all_gather(inputs, "head", axis=1, tiled=True)
    own = call(
        project_kernel,
        jax.ShapeDtypeStruct((B, 2 * HEAD_DIM), bf16),
        (rows, w_key, w_value, v_bias.reshape(1, HEAD_DIM)),
        scratch=(
            pltpu.VMEM(w_key.shape, bf16),
            pltpu.VMEM(w_value.shape, bf16),
            pltpu.VMEM((1, HEAD_DIM), bf16),
            pltpu.SemaphoreType.DMA((3,)),
        ),
        flops=4 * B * rows.shape[1] * HEAD_DIM,
        hbm=(1, 2, 3),
    )
    sibling = swap(own, count)
    pair = jnp.concatenate([own, sibling], axis=0)
    r1 = shift(pair, count, 64, 32)
    r2 = shift(pair, count, 16, 8)
    r3 = shift(pair, count, 4, 2)
    packed = call(half_kernel, jax.ShapeDtypeStruct((B, 2 * HEAD_DIM), bf16), (r1,))
    packed = call(join_kernel, jax.ShapeDtypeStruct((2 * B, 2 * HEAD_DIM), bf16), (packed, r2))
    packed = call(pack_kernel, jax.ShapeDtypeStruct((4 * B, 2 * HEAD_DIM), bf16), (packed, r3))
    swapped = swap(packed, count)
    attended, query_grad, local, near, far = call(
        attention_kernel,
        (
            jax.ShapeDtypeStruct((B, width), bf16),
            jax.ShapeDtypeStruct((B, width), bf16),
            jax.ShapeDtypeStruct((B, 2 * HEAD_DIM), jnp.float32),
            jax.ShapeDtypeStruct((3 * B, 2 * HEAD_DIM), bf16),
            jax.ShapeDtypeStruct((4 * B, 2 * HEAD_DIM), bf16),
        ),
        (place, queries, cotangent, own, sibling, r1, r2, r3, swapped),
        scratch=(
            pltpu.VMEM((8 * B, HEAD_DIM), bf16),
            pltpu.VMEM((8 * B, HEAD_DIM), bf16),
            pltpu.VMEM((width, 8 * B), bf16),
            pltpu.VMEM((width, 8 * B), bf16),
        ),
        flops=12 * width * 8 * B * HEAD_DIM,
    )
    back = swap(far, count)
    m1 = jnp.concatenate([near[:B], back[:B]], axis=0)
    m2 = jnp.concatenate([near[B : 2 * B], back[B : 2 * B]], axis=0)
    extra = jnp.where(place[0] % 2 == 1, back[3 * B :].astype(jnp.float32), 0.0)
    third = (near[2 * B :].astype(jnp.float32) + extra).astype(bf16)
    m3 = jnp.concatenate([third, back[2 * B : 3 * B]], axis=0)
    a1 = shift(m1, count, -64, -32)
    a2 = shift(m2, count, -16, -8)
    a3 = shift(m3, count, -4, -2)
    across = a1[B:].astype(jnp.float32) + a2[B:].astype(jnp.float32) + a3[B:].astype(jnp.float32)
    last = swap(across.astype(bf16), count)
    terms = call(
        finish_kernel,
        jax.ShapeDtypeStruct((4 * B, width), bf16),
        (place, local, back, a1, a2, a3, last, w_key, w_value),
        flops=4 * B * 4 * width * HEAD_DIM,
    )
    arrived = lax.all_to_all(terms, "head", 0, 0, tiled=True)
    input_grad = call(add_kernel, jax.ShapeDtypeStruct((B, width), bf16), (arrived,))
    return (attended, query_grad, input_grad)


def solution(mesh):
    return jax.shard_map(
        shards,
        mesh=mesh,
        in_specs=(
            P("ctx", "head"),
            P("ctx", "head"),
            P(None, "head"),
            P(None, "head"),
            P("head"),
            P("ctx", "head"),
        ),
        out_specs=(P("ctx", "head"), P("ctx", "head"), P("ctx", "head")),
        check_vma=False,
    )
```

```python
import functools
import math

import jax
import jax.numpy as jnp
from jax import lax
from jax.experimental import pallas as pl
from jax.experimental.pallas import tpu as pltpu
from jax.sharding import PartitionSpec as P

HEAD_DIM = 128
BLOCK = 128
DIMS_NT = (((1,), (1,)), ((), ()))
DIMS_TN = (((0,), (0,)), ((), ()))
DIMS_NN = (((1,), (0,)), ((), ()))
SCALE = 1.0 / math.sqrt(HEAD_DIM)
VMEM = pl.BlockSpec(memory_space=pltpu.VMEM)
SMEM = pl.BlockSpec(memory_space=pltpu.SMEM)


def dot(a, b, dims):
    return lax.dot_general(a, b, dims, preferred_element_type=jnp.float32)


def project_kernel(x_ref, wk_hbm, wv_hbm, bias_hbm, kv_ref, wk, wv, bias, sems):
    pairs = [(wk_hbm, wk), (bias_hbm, bias), (wv_hbm, wv)]
    copies = [pltpu.make_async_copy(a, b, sems.at[i]) for i, (a, b) in enumerate(pairs)]
    for copy in copies:
        copy.start()
    rows = x_ref[...]
    copies[0].wait()
    kv_ref[:, :HEAD_DIM] = dot(rows, wk[...], DIMS_NN).astype(jnp.bfloat16)
    copies[1].wait()
    copies[2].wait()
    values = dot(rows, wv[...], DIMS_NN) + bias[...].astype(jnp.float32)
    kv_ref[:, HEAD_DIM:] = values.astype(jnp.bfloat16)


def half_kernel(r1_ref, out_ref):
    out_ref[...] = r1_ref[BLOCK:, :]


def join_kernel(s1_ref, r2_ref, out_ref):
    out_ref[:BLOCK, :] = s1_ref[...]
    out_ref[BLOCK:, :] = r2_ref[BLOCK:, :]


def pack_kernel(s12_ref, r3_ref, out_ref):
    out_ref[: 2 * BLOCK, :] = s12_ref[...]
    out_ref[2 * BLOCK :, :] = r3_ref[...]


def attention_kernel(
    place_ref, q_ref, c_ref, own_ref, sib_ref, r1_ref, r2_ref, r3_ref, sw_ref,
    att_ref, dq_ref, local_ref, near_ref, far_ref,
    keys, values, weights, dscores,
):
    place = place_ref[0]
    core = lax.rem(place, 2)
    group = q_ref.shape[1] // HEAD_DIM
    B = BLOCK
    first = jnp.where(core == 0, sw_ref[2 * B : 3 * B, :], sib_ref[...])
    parts = [own_ref[...], first, r1_ref[:B, :], r2_ref[:B, :], r3_ref[:B, :]]
    parts += [sw_ref[:B, :], sw_ref[B : 2 * B, :], sw_ref[3 * B :, :]]
    for slot, part in enumerate(parts):
        keys[slot * B : (slot + 1) * B, :] = part[:, :HEAD_DIM]
        values[slot * B : (slot + 1) * B, :] = part[:, HEAD_DIM:]
    near, far = jnp.int32(1) - core, core
    steps = [jnp.int32(1)]
    steps += [lax.shift_left(jnp.int32(1), bit + near) for bit in (5, 3, 1)]
    steps += [lax.shift_left(jnp.int32(1), bit + far) for bit in (5, 3, 1)]
    causal = lax.broadcasted_iota(jnp.int32, (B, B), 0) >= lax.broadcasted_iota(jnp.int32, (B, B), 1)
    penalty = [jnp.where(place >= step, 0.0, -jnp.inf).astype(jnp.float32) for step in steps]
    all_keys = keys[...]
    all_values = values[...]
    for head in range(group):
        cols = slice(head * HEAD_DIM, (head + 1) * HEAD_DIM)
        rows = slice(head * B, (head + 1) * B)
        query = q_ref[:, cols]
        grad = c_ref[:, cols]
        raw = dot(query, all_keys, DIMS_NT) * SCALE
        pieces = [jnp.where(causal, raw[:, :B], -jnp.inf)]
        for slot in range(1, 8):
            pieces.append(raw[:, slot * B : (slot + 1) * B] + penalty[slot - 1])
        scores = jnp.concatenate(pieces, axis=1)
        top = jnp.max(scores, axis=1, keepdims=True)
        raised = jnp.exp(scores - top)
        prob = raised * (1.0 / jnp.sum(raised, axis=1, keepdims=True))
        weight = prob.astype(jnp.bfloat16)
        weights[rows, :] = weight
        attended = dot(weight, all_values, DIMS_NN).astype(jnp.bfloat16)
        att_ref[:, cols] = attended
        delta = jnp.sum(
            grad.astype(jnp.float32) * attended.astype(jnp.float32), axis=1, keepdims=True
        )
        dprob = dot(grad, all_values, DIMS_NT)
        dscore = (prob * (dprob - delta)).astype(jnp.bfloat16)
        dscores[rows, :] = dscore
        dq_ref[:, cols] = (dot(dscore, all_keys, DIMS_NN) * SCALE).astype(jnp.bfloat16)
    queries = jnp.concatenate(
        [q_ref[:, h * HEAD_DIM : (h + 1) * HEAD_DIM] for h in range(group)], axis=0
    )
    grads = jnp.concatenate(
        [c_ref[:, h * HEAD_DIM : (h + 1) * HEAD_DIM] for h in range(group)], axis=0
    )
    for slot in range(8):
        cols = slice(slot * B, (slot + 1) * B)
        dkey = dot(dscores[:, cols], queries, DIMS_TN) * SCALE
        dvalue = dot(weights[:, cols], grads, DIMS_TN)
        if slot == 0:
            local_ref[:, :HEAD_DIM] = dkey
            local_ref[:, HEAD_DIM:] = dvalue
        else:
            target, row = (near_ref, slot - 2) if 2 <= slot < 5 else (far_ref, slot - 5)
            if slot == 1:
                target, row = far_ref, 3
            target[row * B : (row + 1) * B, :HEAD_DIM] = dkey.astype(jnp.bfloat16)
            target[row * B : (row + 1) * B, HEAD_DIM:] = dvalue.astype(jnp.bfloat16)


def total_kernel(place_ref, local_ref, swap_ref, a1_ref, a2_ref, a3_ref, t_ref, out_ref):
    core = lax.rem(place_ref[0], 2)
    B = BLOCK
    total = local_ref[...]
    total += jnp.where(core == 0, swap_ref[3 * B :, :].astype(jnp.float32), 0.0)
    for ref in (a1_ref, a2_ref, a3_ref):
        total += ref[:B, :].astype(jnp.float32)
    total = (total + t_ref[...].astype(jnp.float32)).astype(jnp.bfloat16)
    for part in range(4):
        out_ref[part * B : (part + 1) * B, :] = total


def finish_kernel(grads_ref, slabs_ref, out_ref):
    B = BLOCK
    total = jnp.zeros(out_ref.shape, jnp.float32)
    for part in range(4):
        for side in range(2):
            grads = grads_ref[part * B : (part + 1) * B, side * HEAD_DIM : (side + 1) * HEAD_DIM]
            total += dot(grads, slabs_ref[part, side], DIMS_NT)
    out_ref[...] = total.astype(jnp.bfloat16)


def out_spec(shape):
    return VMEM if isinstance(shape, jax.ShapeDtypeStruct) else pl.BlockSpec(memory_space=pltpu.HBM)


def call(kernel, out_shape, args, scratch=(), flops=0, hbm=()):
    specs = [SMEM if a.dtype == jnp.int32 else VMEM for a in args]
    for index in hbm:
        specs[index] = pl.BlockSpec(memory_space=pltpu.HBM)
    args = [
        pltpu.with_memory_space_constraint(a, pltpu.HBM) if i in hbm else a
        for i, a in enumerate(args)
    ]
    return pl.pallas_call(
        kernel,
        out_shape=out_shape,
        in_specs=specs,
        out_specs=jax.tree.map(out_spec, out_shape),
        scratch_shapes=list(scratch),
        compiler_params=pltpu.CompilerParams(vmem_limit_bytes=30 * 1024 * 1024),
        cost_estimate=pl.CostEstimate(
            flops=flops,
            bytes_accessed=sum(a.size * a.dtype.itemsize for a in args),
            transcendentals=0,
        ),
    )(*args)


def swap(value, count):
    return lax.ppermute(value, "ctx", [(i, i ^ 1) for i in range(count)])


def shift(value, count, even, odd):
    pairs = []
    for i in range(count):
        to = i + (even if i % 2 == 0 else odd)
        if 0 <= to < count:
            pairs.append((i, to))
    return lax.ppermute(value, "ctx", pairs)


def shards(inputs, queries, w_key, w_value, v_bias, cotangent):
    count = lax.axis_size("ctx")
    place = lax.axis_index("ctx").astype(jnp.int32).reshape(1)
    B = BLOCK
    bf16 = jnp.bfloat16
    width = queries.shape[1]
    rows = lax.all_gather(inputs, "head", axis=1, tiled=True)
    own = call(
        project_kernel,
        jax.ShapeDtypeStruct((B, 2 * HEAD_DIM), bf16),
        (rows, w_key, w_value, v_bias.reshape(1, HEAD_DIM)),
        scratch=(
            pltpu.VMEM(w_key.shape, bf16),
            pltpu.VMEM(w_value.shape, bf16),
            pltpu.VMEM((1, HEAD_DIM), bf16),
            pltpu.SemaphoreType.DMA((3,)),
        ),
        flops=4 * B * rows.shape[1] * HEAD_DIM,
        hbm=(1, 2, 3),
    )
    sibling = swap(own, count)
    pair = jnp.concatenate([own, sibling], axis=0)
    depth = w_key.shape[0] // 4
    slab_shape = (4, depth, HEAD_DIM)
    key_rows, value_rows, pair = lax.optimization_barrier((w_key, w_value, pair))
    slabs = jnp.stack([key_rows.reshape(slab_shape), value_rows.reshape(slab_shape)], axis=1)
    r1 = shift(pair, count, 64, 32)
    r2 = shift(pair, count, 16, 8)
    r3 = shift(pair, count, 4, 2)
    packed = call(half_kernel, jax.ShapeDtypeStruct((B, 2 * HEAD_DIM), bf16), (r1,))
    packed = call(join_kernel, jax.ShapeDtypeStruct((2 * B, 2 * HEAD_DIM), bf16), (packed, r2))
    packed = call(pack_kernel, jax.ShapeDtypeStruct((4 * B, 2 * HEAD_DIM), bf16), (packed, r3))
    swapped = swap(packed, count)
    attended, query_grad, local, near, far = call(
        attention_kernel,
        (
            jax.ShapeDtypeStruct((B, width), bf16),
            jax.ShapeDtypeStruct((B, width), bf16),
            jax.ShapeDtypeStruct((B, 2 * HEAD_DIM), jnp.float32),
            jax.ShapeDtypeStruct((3 * B, 2 * HEAD_DIM), bf16),
            jax.ShapeDtypeStruct((4 * B, 2 * HEAD_DIM), bf16),
        ),
        (place, queries, cotangent, own, sibling, r1, r2, r3, swapped),
        scratch=(
            pltpu.VMEM((8 * B, HEAD_DIM), bf16),
            pltpu.VMEM((8 * B, HEAD_DIM), bf16),
            pltpu.VMEM((width, 8 * B), bf16),
            pltpu.VMEM((width, 8 * B), bf16),
        ),
        flops=12 * width * 8 * B * HEAD_DIM,
    )
    far, slabs = lax.optimization_barrier((far, slabs))
    slabs = lax.all_to_all(slabs, "head", 0, 0, tiled=True)
    back = swap(far, count)
    m1 = jnp.concatenate([near[:B], back[:B]], axis=0)
    m2 = jnp.concatenate([near[B : 2 * B], back[B : 2 * B]], axis=0)
    extra = jnp.where(place[0] % 2 == 1, back[3 * B :].astype(jnp.float32), 0.0)
    third = (near[2 * B :].astype(jnp.float32) + extra).astype(bf16)
    m3 = jnp.concatenate([third, back[2 * B : 3 * B]], axis=0)
    a1 = shift(m1, count, -64, -32)
    a2 = shift(m2, count, -16, -8)
    a3 = shift(m3, count, -4, -2)
    across = a1[B:].astype(jnp.float32) + a2[B:].astype(jnp.float32) + a3[B:].astype(jnp.float32)
    last = swap(across.astype(bf16), count)
    last, slabs = lax.optimization_barrier((last, slabs))
    total = call(
        total_kernel,
        jax.ShapeDtypeStruct((4 * B, 2 * HEAD_DIM), bf16),
        (place, local, back, a1, a2, a3, last),
    )
    arrived = lax.all_to_all(total, "head", 0, 0, tiled=True)
    input_grad = call(
        finish_kernel,
        jax.ShapeDtypeStruct((B, width), bf16),
        (arrived, slabs),
        flops=16 * B * width * HEAD_DIM,
    )
    return (attended, query_grad, input_grad)


def solution(mesh):
    return jax.shard_map(
        shards,
        mesh=mesh,
        in_specs=(
            P("ctx", "head"),
            P("ctx", "head"),
            P(None, "head"),
            P(None, "head"),
            P("head"),
            P("ctx", "head"),
        ),
        out_specs=(P("ctx", "head"), P("ctx", "head"), P("ctx", "head")),
        check_vma=False,
    )
```

```python
import functools
import math

import jax
import jax.numpy as jnp
from jax import lax
from jax.experimental import pallas as pl
from jax.experimental.pallas import tpu as pltpu
from jax.sharding import Mesh
from jax.sharding import PartitionSpec as P

HEAD_DIM = 128
BLOCK = 128
CTX = ("pair", "core")
DIMS_NT = (((1,), (1,)), ((), ()))
DIMS_TN = (((0,), (0,)), ((), ()))
DIMS_NN = (((1,), (0,)), ((), ()))
SCALE = 1.0 / math.sqrt(HEAD_DIM)
VMEM = pl.BlockSpec(memory_space=pltpu.VMEM)
SMEM = pl.BlockSpec(memory_space=pltpu.SMEM)


def dot(a, b, dims):
    return lax.dot_general(a, b, dims, preferred_element_type=jnp.float32)


def project_kernel(x_ref, wk_hbm, wv_hbm, bias_hbm, kv_ref, wk, wv, bias, sems):
    pairs = [(wk_hbm, wk), (bias_hbm, bias), (wv_hbm, wv)]
    copies = [pltpu.make_async_copy(a, b, sems.at[i]) for i, (a, b) in enumerate(pairs)]
    for copy in copies:
        copy.start()
    rows = x_ref[...]
    copies[0].wait()
    kv_ref[:, :HEAD_DIM] = dot(rows, wk[...], DIMS_NN).astype(jnp.bfloat16)
    copies[1].wait()
    copies[2].wait()
    values = dot(rows, wv[...], DIMS_NN) + bias[...].astype(jnp.float32)
    kv_ref[:, HEAD_DIM:] = values.astype(jnp.bfloat16)


def half_kernel(r1_ref, out_ref):
    out_ref[...] = r1_ref[BLOCK:, :]


def join_kernel(s1_ref, r2_ref, out_ref):
    out_ref[:BLOCK, :] = s1_ref[...]
    out_ref[BLOCK:, :] = r2_ref[BLOCK:, :]


def pack_kernel(s12_ref, r3_ref, out_ref):
    out_ref[: 2 * BLOCK, :] = s12_ref[...]
    out_ref[2 * BLOCK :, :] = r3_ref[...]


def attention_kernel(
    place_ref, q_ref, c_ref, own_ref, sib_ref, r1_ref, r2_ref, r3_ref, sw_ref,
    att_ref, dq_ref, local_ref, near_ref, far_ref,
    keys, values, weights, dscores,
):
    place = place_ref[0]
    core = lax.rem(place, 2)
    group = q_ref.shape[1] // HEAD_DIM
    B = BLOCK
    first = jnp.where(core == 0, sw_ref[2 * B : 3 * B, :], sib_ref[...])
    parts = [own_ref[...], first, r1_ref[:B, :], r2_ref[:B, :], r3_ref[:B, :]]
    parts += [sw_ref[:B, :], sw_ref[B : 2 * B, :], sw_ref[3 * B :, :]]
    for slot, part in enumerate(parts):
        keys[slot * B : (slot + 1) * B, :] = part[:, :HEAD_DIM]
        values[slot * B : (slot + 1) * B, :] = part[:, HEAD_DIM:]
    near, far = jnp.int32(1) - core, core
    steps = [jnp.int32(1)]
    steps += [lax.shift_left(jnp.int32(1), bit + near) for bit in (5, 3, 1)]
    steps += [lax.shift_left(jnp.int32(1), bit + far) for bit in (5, 3, 1)]
    causal = lax.broadcasted_iota(jnp.int32, (B, B), 0) >= lax.broadcasted_iota(jnp.int32, (B, B), 1)
    penalty = [jnp.where(place >= step, 0.0, -jnp.inf).astype(jnp.float32) for step in steps]
    all_keys = keys[...]
    all_values = values[...]
    for head in range(group):
        cols = slice(head * HEAD_DIM, (head + 1) * HEAD_DIM)
        rows = slice(head * B, (head + 1) * B)
        query = q_ref[:, cols]
        grad = c_ref[:, cols]
        raw = dot(query, all_keys, DIMS_NT) * SCALE
        pieces = [jnp.where(causal, raw[:, :B], -jnp.inf)]
        for slot in range(1, 8):
            pieces.append(raw[:, slot * B : (slot + 1) * B] + penalty[slot - 1])
        scores = jnp.concatenate(pieces, axis=1)
        top = jnp.max(scores, axis=1, keepdims=True)
        raised = jnp.exp(scores - top)
        prob = raised * (1.0 / jnp.sum(raised, axis=1, keepdims=True))
        weight = prob.astype(jnp.bfloat16)
        weights[rows, :] = weight
        attended = dot(weight, all_values, DIMS_NN).astype(jnp.bfloat16)
        att_ref[:, cols] = attended
        delta = jnp.sum(
            grad.astype(jnp.float32) * attended.astype(jnp.float32), axis=1, keepdims=True
        )
        dprob = dot(grad, all_values, DIMS_NT)
        dscore = (prob * (dprob - delta)).astype(jnp.bfloat16)
        dscores[rows, :] = dscore
        dq_ref[:, cols] = (dot(dscore, all_keys, DIMS_NN) * SCALE).astype(jnp.bfloat16)
    queries = jnp.concatenate(
        [q_ref[:, h * HEAD_DIM : (h + 1) * HEAD_DIM] for h in range(group)], axis=0
    )
    grads = jnp.concatenate(
        [c_ref[:, h * HEAD_DIM : (h + 1) * HEAD_DIM] for h in range(group)], axis=0
    )
    for slot in range(8):
        cols = slice(slot * B, (slot + 1) * B)
        dkey = dot(dscores[:, cols], queries, DIMS_TN) * SCALE
        dvalue = dot(weights[:, cols], grads, DIMS_TN)
        if slot == 0:
            local_ref[:, :HEAD_DIM] = dkey
            local_ref[:, HEAD_DIM:] = dvalue
        else:
            target, row = (near_ref, slot - 2) if 2 <= slot < 5 else (far_ref, slot - 5)
            if slot == 1:
                target, row = far_ref, 3
            target[row * B : (row + 1) * B, :HEAD_DIM] = dkey.astype(jnp.bfloat16)
            target[row * B : (row + 1) * B, HEAD_DIM:] = dvalue.astype(jnp.bfloat16)


def total_kernel(place_ref, local_ref, swap_ref, a1_ref, a2_ref, a3_ref, out_ref):
    core = lax.rem(place_ref[0], 2)
    B = BLOCK
    total = local_ref[...]
    total += jnp.where(core == 0, swap_ref[3 * B :, :].astype(jnp.float32), 0.0)
    across = jnp.zeros(total.shape, jnp.float32)
    for ref in (a1_ref, a2_ref, a3_ref):
        total += ref[:B, :].astype(jnp.float32)
        across += ref[B:, :].astype(jnp.float32)
    for side in range(2):
        value = jnp.where(core == side, total, across).astype(jnp.bfloat16)
        for part in range(4):
            row = (side * 4 + part) * B
            out_ref[row : row + B, :] = value


def finish_kernel(grads_ref, slabs_ref, out_ref):
    B = BLOCK
    total = jnp.zeros(out_ref.shape, jnp.float32)
    for part in range(4):
        even = grads_ref[part * B : (part + 1) * B, :].astype(jnp.float32)
        odd = grads_ref[(part + 4) * B : (part + 5) * B, :].astype(jnp.float32)
        grads = (even + odd).astype(jnp.bfloat16)
        for side in range(2):
            half = grads[:, side * HEAD_DIM : (side + 1) * HEAD_DIM]
            total += dot(half, slabs_ref[part, side], DIMS_NT)
    out_ref[...] = total.astype(jnp.bfloat16)


def out_spec(shape):
    return VMEM if isinstance(shape, jax.ShapeDtypeStruct) else pl.BlockSpec(memory_space=pltpu.HBM)


def call(kernel, out_shape, args, scratch=(), flops=0, hbm=()):
    specs = [SMEM if a.dtype == jnp.int32 else VMEM for a in args]
    for index in hbm:
        specs[index] = pl.BlockSpec(memory_space=pltpu.HBM)
    args = [
        pltpu.with_memory_space_constraint(a, pltpu.HBM) if i in hbm else a
        for i, a in enumerate(args)
    ]
    return pl.pallas_call(
        kernel,
        out_shape=out_shape,
        in_specs=specs,
        out_specs=jax.tree.map(out_spec, out_shape),
        scratch_shapes=list(scratch),
        compiler_params=pltpu.CompilerParams(vmem_limit_bytes=30 * 1024 * 1024),
        cost_estimate=pl.CostEstimate(
            flops=flops,
            bytes_accessed=sum(a.size * a.dtype.itemsize for a in args),
            transcendentals=0,
        ),
    )(*args)


def swap(value, count):
    return lax.ppermute(value, CTX, [(i, i ^ 1) for i in range(count)])


def shift(value, count, even, odd):
    pairs = []
    for i in range(count):
        to = i + (even if i % 2 == 0 else odd)
        if 0 <= to < count:
            pairs.append((i, to))
    return lax.ppermute(value, CTX, pairs)


def shards(inputs, queries, w_key, w_value, v_bias, cotangent):
    count = lax.axis_size("pair") * 2
    place = lax.axis_index(CTX).astype(jnp.int32).reshape(1)
    B = BLOCK
    bf16 = jnp.bfloat16
    width = queries.shape[1]
    rows = lax.all_gather(inputs, "head", axis=1, tiled=True)
    own = call(
        project_kernel,
        jax.ShapeDtypeStruct((B, 2 * HEAD_DIM), bf16),
        (rows, w_key, w_value, v_bias.reshape(1, HEAD_DIM)),
        scratch=(
            pltpu.VMEM(w_key.shape, bf16),
            pltpu.VMEM(w_value.shape, bf16),
            pltpu.VMEM((1, HEAD_DIM), bf16),
            pltpu.SemaphoreType.DMA((3,)),
        ),
        flops=4 * B * rows.shape[1] * HEAD_DIM,
        hbm=(1, 2, 3),
    )
    sibling = swap(own, count)
    pair = jnp.concatenate([own, sibling], axis=0)
    depth = w_key.shape[0] // 4
    slab_shape = (4, depth, HEAD_DIM)
    key_rows, value_rows, pair = lax.optimization_barrier((w_key, w_value, pair))
    slabs = jnp.stack([key_rows.reshape(slab_shape), value_rows.reshape(slab_shape)], axis=1)
    r1 = shift(pair, count, 64, 32)
    r2 = shift(pair, count, 16, 8)
    r3 = shift(pair, count, 4, 2)
    packed = call(half_kernel, jax.ShapeDtypeStruct((B, 2 * HEAD_DIM), bf16), (r1,))
    packed = call(join_kernel, jax.ShapeDtypeStruct((2 * B, 2 * HEAD_DIM), bf16), (packed, r2))
    packed = call(pack_kernel, jax.ShapeDtypeStruct((4 * B, 2 * HEAD_DIM), bf16), (packed, r3))
    swapped = swap(packed, count)
    attended, query_grad, local, near, far = call(
        attention_kernel,
        (
            jax.ShapeDtypeStruct((B, width), bf16),
            jax.ShapeDtypeStruct((B, width), bf16),
            jax.ShapeDtypeStruct((B, 2 * HEAD_DIM), jnp.float32),
            jax.ShapeDtypeStruct((3 * B, 2 * HEAD_DIM), bf16),
            jax.ShapeDtypeStruct((4 * B, 2 * HEAD_DIM), bf16),
        ),
        (place, queries, cotangent, own, sibling, r1, r2, r3, swapped),
        scratch=(
            pltpu.VMEM((8 * B, HEAD_DIM), bf16),
            pltpu.VMEM((8 * B, HEAD_DIM), bf16),
            pltpu.VMEM((width, 8 * B), bf16),
            pltpu.VMEM((width, 8 * B), bf16),
        ),
        flops=12 * width * 8 * B * HEAD_DIM,
    )
    far, slabs = lax.optimization_barrier((far, slabs))
    slabs = lax.all_to_all(slabs, "head", 0, 0, tiled=True)
    back = swap(far, count)
    m1 = jnp.concatenate([near[:B], back[:B]], axis=0)
    m2 = jnp.concatenate([near[B : 2 * B], back[B : 2 * B]], axis=0)
    extra = jnp.where(place[0] % 2 == 1, back[3 * B :].astype(jnp.float32), 0.0)
    third = (near[2 * B :].astype(jnp.float32) + extra).astype(bf16)
    m3 = jnp.concatenate([third, back[2 * B : 3 * B]], axis=0)
    a1 = shift(m1, count, -64, -32)
    a2 = shift(m2, count, -16, -8)
    a3 = shift(m3, count, -4, -2)
    total = call(
        total_kernel,
        jax.ShapeDtypeStruct((8 * B, 2 * HEAD_DIM), bf16),
        (place, local, back, a1, a2, a3),
    )
    total, slabs = lax.optimization_barrier((total, slabs))
    arrived = lax.all_to_all(total, ("core", "head"), 0, 0, tiled=True)
    input_grad = call(
        finish_kernel,
        jax.ShapeDtypeStruct((B, width), bf16),
        (arrived, slabs),
        flops=16 * B * width * HEAD_DIM,
    )
    return (attended, query_grad, input_grad)


def solution(mesh):
    return jax.shard_map(
        shards,
        mesh=Mesh(mesh.devices.reshape(-1, 2, mesh.devices.shape[1]), ("pair", "core", "head")),
        in_specs=(
            P(CTX, "head"),
            P(CTX, "head"),
            P(None, "head"),
            P(None, "head"),
            P("head"),
            P(CTX, "head"),
        ),
        out_specs=(P(CTX, "head"), P(CTX, "head"), P(CTX, "head")),
        check_vma=False,
    )
```
